512 devices in a mesh: gx: 4 (over z_lo, core), gy: 32 (over z_hi, y), gz: 4 (over x).
Axes of the slice: x: 4, y: 8, z: 8 (z_hi: 4, z_lo: 2; z = z_hi * 2 + z_lo), core: 2. Of those that a mesh axis runs over, the one named last changes fastest.
Arguments:
- cell_state: float32 [3, 32, 512, 512], P(None, 'gx', 'gy', 'gz'), may hold values from 0 to 1, as said below
- old_mass: float32 [3, 32, 512, 512], P(None, 'gx', 'gy', 'gz'), may hold values from 0 to 1.5
- pore_volume: float32 [32, 512, 512], P('gx', 'gy', 'gz'), may hold values from 0.5 to 2
- transmissibility: float32 [13, 32, 512, 512], P(None, 'gx', 'gy', 'gz'), may hold values from 0.02 to 1
- active_mask: int32 [32, 512, 512], P('gx', 'gy', 'gz'), may hold values 0 or 1
- pvt_region: int32 [32, 512, 512], P('gx', 'gy', 'gz'), may hold values from 0 to 7
- formation_factor: float32 [3, 8], replicated, may hold values from 0.6 to 1.5
- compressibility: float32 [3, 8], replicated, may hold values from 0.05 to 0.2
- inverse_viscosity: float32 [3, 8], replicated, may hold values from 0.3 to 3
Outputs:
- residual: float32 [3, 32, 512, 512], P(None, 'gx', 'gy', 'gz')
- pressure_update: float32 [32, 512, 512], P('gx', 'gy', 'gz')
The draws below stay inside these ranges and needn't reach their ends.
Inputs may be any that keep to these rules, and one draw needn't show every extreme that they name: `cell_state`: channel 0 is the pressure; channels 1 and 2 are positive saturations whose sum stays below 1.
All inputs are finite; a program needn't handle non-finite values. No bound on the sum of `active_mask` on one device may be relied on, other than what follows from the above.
Results may differ from the reference program's by a relative error of at most 0.0003.
Values sent between devices are 32-bit elements; how exact they have to be, the bound alone decides.
A program may use at most 64 MiB of HBM per device.

```python
import math
import jax
import jax.numpy as jnp

REGIONS = 8
SWEEPS = 4
NX = 32
NY = 512
NZ = 512


def draw_cell_state(key, part):
    key_pressure, key_water, key_oil, key_gas = jax.random.split(key, 4)
    shape_cells = (NX, NY, NZ)
    pressure = jax.random.uniform(key_pressure, shape_cells, jnp.float32, 0.0, 1.0)
    water_part = jnp.exp(jax.random.uniform(key_water, shape_cells, jnp.float32, -1.0, 1.0))
    oil_part = jnp.exp(jax.random.uniform(key_oil, shape_cells, jnp.float32, -1.0, 1.0))
    gas_part = jnp.exp(jax.random.uniform(key_gas, shape_cells, jnp.float32, -1.0, 1.0))
    part_sum = water_part + oil_part + gas_part
    return jnp.stack([pressure, water_part / part_sum, gas_part / part_sum]).astype(jnp.float32)


def plant(entries, own_key, smallest, high):
    shape = entries.shape
    spot = [jax.random.randint(jax.random.fold_in(own_key, axis), (), 0, shape[axis]) for axis in range(len(shape))]
    entries = entries.at[tuple(spot)].set(smallest)
    longest = shape.index(max(shape))
    spot[longest] = (spot[longest] + 1) % shape[longest]
    return entries.at[tuple(spot)].set(high)


def block_scale(stream_key, shape, pieces, low, top_value):
    level, own = 1.0, jax.random.fold_in(stream_key, 6)
    for dim, blocks in pieces:
        steps = jnp.exp(jax.random.uniform(jax.random.fold_in(own, dim), (blocks,), jnp.float32, low / len(pieces), top_value / len(pieces)))
        level = level * jnp.repeat(steps, shape[dim] // blocks).reshape([-1 if axis == dim else 1 for axis in range(len(shape))])
    return level


def setup_inputs(seed: int = 0) -> dict:
    key_list = jax.random.split(jax.random.key(seed), 10)
    return {
        "cell_state": draw_cell_state(jax.random.fold_in(key_list[9], 71), 0),
        "old_mass": jnp.clip(1.5 * jax.random.uniform(key_list[1], (3, NX, NY, NZ), jnp.float32) ** block_scale(key_list[1], (3, NX, NY, NZ), ((1, 4), (2, 32), (3, 4)), -0.2, 0.2), 0.0, 1.5),
        "pore_volume": jnp.clip(jnp.exp(math.log(2.0) - 1.3862944 * jax.random.uniform(key_list[2], (NX, NY, NZ), jnp.float32) ** block_scale(key_list[2], (NX, NY, NZ), ((0, 4), (1, 32), (2, 4)), -0.2, 0.2)), 0.5, 2.0),
        "transmissibility": jnp.clip(jnp.exp(math.log(1.0) - 3.912023 * jax.random.uniform(key_list[3], (13, NX, NY, NZ), jnp.float32) ** block_scale(key_list[3], (13, NX, NY, NZ), ((1, 4), (2, 32), (3, 4)), -0.2, 0.2)), 0.02, 1.0),
        "active_mask": plant((jax.random.randint(key_list[4], (NX, NY, NZ), 0, 10) < 9).astype(jnp.int32), jax.random.fold_in(key_list[4], 1), 0, 1),
        "pvt_region": plant(jax.random.randint(key_list[5], (NX, NY, NZ), 0, REGIONS), jax.random.fold_in(key_list[5], 1), 0, REGIONS - 1).astype(jnp.int32),
        "formation_factor": jnp.clip(jnp.exp(jax.random.uniform(key_list[6], (3, REGIONS), jnp.float32, math.log(0.6), math.log(1.5))), 0.6, 1.5),
        "compressibility": jnp.clip(jnp.exp(jax.random.uniform(key_list[7], (3, REGIONS), jnp.float32, math.log(0.05), math.log(0.2))), 0.05, 0.2),
        "inverse_viscosity": jnp.clip(jnp.exp(jax.random.uniform(key_list[8], (3, REGIONS), jnp.float32, math.log(0.3), math.log(3.0))), 0.3, 3.0),
    }


neighbour_offsets = [(along_x, along_y, along_z) for along_x in (-1, 0, 1) for along_y in (-1, 0, 1) for along_z in (-1, 0, 1) if (along_x, along_y, along_z) != (0, 0, 0)]
upper_offsets = [offset for offset in neighbour_offsets if offset > (0, 0, 0)]
relax_weight = 0.7


def window(values_in, offset):
    extent = values_in.shape[-3:]
    return values_in[..., 1 + offset[0]:extent[0] - 1 + offset[0], 1 + offset[1]:extent[1] - 1 + offset[1], 1 + offset[2]:extent[2] - 1 + offset[2]]


def lookup(table_in, region_float):
    looked_up = jnp.zeros((table_in.shape[0],) + region_float.shape, region_float.dtype)
    for level in range(table_in.shape[1]):
        chosen = (region_float == level).astype(region_float.dtype)
        looked_up = looked_up + table_in[:, level][:, None, None, None] * chosen[None]
    return looked_up


def assemble(padded, old_mass, pore_volume, tables):
    formation, compress_table, viscous_inverse = tables
    pressure = padded[0]
    active = padded[3]
    saturation = jnp.stack([padded[1], 1.0 - padded[1] - padded[2], padded[2]])
    compress_rate = lookup(compress_table, padded[4])
    expansion = lookup(formation, padded[4]) * jnp.exp(compress_rate * (pressure[None] - 0.5))
    mobility = lookup(viscous_inverse, padded[4]) * expansion * saturation * saturation
    slope_all = compress_rate * mobility
    centre = (0, 0, 0)
    press_here = window(pressure, centre)
    active_here = window(active, centre)
    mobility_here = window(mobility, centre)
    slope_here = window(slope_all, centre)
    saturation_here = window(saturation, centre)
    expansion_here = window(expansion, centre)
    storage = pore_volume * jnp.sum(window(compress_rate, centre) * saturation_here, axis=0)
    scaling = 1.0 / jnp.where(active_here > 0, storage, 1.0)
    weights = scaling[None] / expansion_here
    flux_total = jnp.zeros_like(saturation_here)
    diagonal = jnp.ones_like(press_here)
    couplings = []
    for offset in neighbour_offsets:
        if offset in upper_offsets:
            link_trans = window(padded[5 + upper_offsets.index(offset)], centre)
        else:
            mirror = (-offset[0], -offset[1], -offset[2])
            link_trans = window(padded[5 + upper_offsets.index(mirror)], offset)
        link_trans = link_trans * active_here * window(active, offset)
        press_drop = press_here - window(pressure, offset)
        mobility_mean = 0.5 * (mobility_here + window(mobility, offset))
        flux_total = flux_total + link_trans * mobility_mean * press_drop
        diagonal = diagonal + link_trans * jnp.sum(weights * (0.5 * slope_here * press_drop + mobility_mean), axis=0)
        couplings.append(link_trans * jnp.sum(weights * (0.5 * window(slope_all, offset) * press_drop - mobility_mean), axis=0))
    residual = active_here * (pore_volume * expansion_here * saturation_here - old_mass + flux_total)
    pressure_rhs = -jnp.sum(weights * residual, axis=0)
    return residual, diagonal, jnp.stack(couplings), pressure_rhs


def relax(padded_update, diagonal, couplings, pressure_rhs):
    centre_update = window(padded_update, (0, 0, 0))
    product = diagonal * centre_update
    for position, offset in enumerate(neighbour_offsets):
        product = product + couplings[position] * window(padded_update, offset)
    return centre_update + relax_weight * (pressure_rhs - product) / diagonal


def reference(cell_state, old_mass, pore_volume, transmissibility, active_mask, pvt_region, formation_factor, compressibility, inverse_viscosity):
    stacked = jnp.concatenate([cell_state, active_mask[None].astype(cell_state.dtype), pvt_region[None].astype(cell_state.dtype), transmissibility], axis=0)
    padded = jnp.pad(stacked, ((0, 0), (1, 1), (1, 1), (1, 1)))
    residual, diagonal, couplings, pressure_rhs = assemble(padded, old_mass, pore_volume, (formation_factor, compressibility, inverse_viscosity))
    update = relax_weight * pressure_rhs / diagonal
    for sweep_index in range(SWEEPS - 1):
        update = relax(jnp.pad(update, 1), diagonal, couplings, pressure_rhs)
    return residual, update
```

```python
import functools
import itertools

import jax
import jax.numpy as jnp
from jax import lax
from jax.experimental import pallas as pl
from jax.experimental.pallas import tpu as pltpu
from jax.sharding import PartitionSpec as P

MESH = pl.DeviceIdType.MESH
F32 = jnp.float32
AXES = ("gx", "gy", "gz")
relax_weight = 0.7

offsets = [o for o in itertools.product((-1, 0, 1), repeat=3) if o != (0, 0, 0)]
upper = [o for o in offsets if o > (0, 0, 0)]
minus = lambda o: (-o[0], -o[1], -o[2])

OM, PV, PR, SW, SG, AM, RG = 0, 3, 11, 12, 13, 14, 15
TCH = {4: 4, 5: 5, 6: 6, 7: 7, 8: 8, 9: 9, 0: 10, 10: 16, 11: 17, 12: 18, 1: 19, 2: 20, 3: 21}
NCH = 22
X_LOW, X_HIGH = (4, 19), (11, 16)
Y_LOW, Y_LOW2, Y_HIGH = (7, 22), (11, 22), (4, 16)
REST_LOW, REST_HIGH = ((0, 7),), ((0, 4), (16, 22))

NP, NR = 10, 32
T_ROLLED = [k for k, o in enumerate(upper) if o[2] != 0]
PACKED = [PR, SW, SG, AM, RG] + [TCH[k] for k in T_ROLLED]


def rows_sent(dy, wide):
    if dy == 0:
        return (7, 25) if wide else (8, 24), (7, 25) if wide else (8, 24)
    if dy > 0:
        return (22, 24), (6, 8)
    return (8, 10), (24, 26)


def kernel(
    cs, om, pv, tr, am, rg, b_hbm, c_hbm, v_hbm,
    res_out, x_out,
    b_tab, c_tab, v_tab, ext, ints, fld, tl, wts, base, acoef, dinv, xs, px, zx, pk, zb, zf,
    in_sem, s_state, r_state, s_rest, r_rest, s_x, r_x,
):
    me = [lax.axis_index(a) for a in AXES]
    dims = [lax.axis_size(a) for a in AXES]

    def present(o):
        cond = None
        for i, s in enumerate(o):
            if s:
                here = me[i] + s >= 0 if s < 0 else me[i] + s < dims[i]
                cond = here if cond is None else cond & here
        return cond

    def device(o):
        return tuple(jnp.clip(me[i] + s, 0, dims[i] - 1) if s else me[i] for i, s in enumerate(o))

    loads = [
        (cs, ext.at[PR : PR + 3, 1:9, 8:24]),
        (om, ext.at[OM : OM + 3, 1:9, 8:24]),
        (pv, ext.at[PV, 1:9, 8:24]),
        (am, ints.at[0]),
        (rg, ints.at[1]),
        (tr.at[0], ext.at[10, 1:9, 8:24]),
        (tr.at[4:10], ext.at[4:10, 1:9, 8:24]),
        (tr.at[10:13], ext.at[16:19, 1:9, 8:24]),
        (tr.at[1:4], ext.at[19:22, 1:9, 8:24]),
        (b_hbm, b_tab),
        (c_hbm, c_tab),
        (v_hbm, v_tab),
    ]
    copies = [pltpu.make_async_copy(a, b, in_sem.at[i]) for i, (a, b) in enumerate(loads)]
    for c in copies:
        c.start()

    first = [me[i] == 0 for i in range(3)]
    last = [me[i] == dims[i] - 1 for i in range(3)]

    def zero(ref):
        ref[...] = jnp.zeros(ref.shape, ref.dtype)

    @pl.when(first[0])
    def _():
        zero(ext.at[4:19, 0])

    @pl.when(last[0])
    def _():
        zero(ext.at[11:16, 9])

    @pl.when(first[1])
    def _():
        zero(ext.at[:, :, 0:8])

    @pl.when(last[1])
    def _():
        zero(ext.at[:, :, 24:32])

    border = first[0] | first[1] | first[2] | last[0] | last[1] | last[2]

    @pl.when(border)
    def _():
        zero(zb)
        zero(zx)
        for n in range(3):
            zero(xs.at[n, 1])

    barrier = pltpu.get_barrier_semaphore()
    for o in offsets:

        @pl.when(present(o))
        def _(o=o):
            pl.semaphore_signal(barrier, inc=1, device_id=device(o), device_id_type=MESH)

    for c in copies:
        c.wait()

    def convert(i, carry):
        ext[AM, i + 1, 8:24] = ints[0, i].astype(F32)
        ext[RG, i + 1, 8:24] = ints[1, i].astype(F32)
        return carry

    lax.fori_loop(0, 8, convert, 0)

    lane16 = lax.broadcasted_iota(jnp.int32, (16, 128), 1)
    lane24 = lax.broadcasted_iota(jnp.int32, (24, 128), 1)
    even24 = lane24 % 2 == 0

    def pack(x, accs):
        accs = list(accs)
        for s, ch in enumerate(PACKED):
            to = 16 * (s % 8) + 2 * x
            moved = pltpu.roll(ext[ch, x + 1, 8:24], to + 1, 1)
            accs[s // 8] = jnp.where((lane16 == to) | (lane16 == to + 1), moved, accs[s // 8])
        return tuple(accs)

    packed = lax.fori_loop(0, 8, pack, (jnp.zeros((16, 128), F32),) * 2)
    for k in range(2):
        pk[k, 8:24] = packed[k]

    peers = 1
    for i in range(3):
        peers = peers * (1 + (me[i] > 0).astype(jnp.int32) + (me[i] < dims[i] - 1).astype(jnp.int32))
    pl.semaphore_wait(barrier, peers - 1)

    def messages_state():
        found = []
        for dy, (lo, hi), row, to in (
            (1, Y_LOW, 23, 7),
            (-1, Y_HIGH, 8, 24),
            (1, Y_LOW2, 22, 6),
            (-1, Y_HIGH, 9, 25),
        ):
            found.append(((0, dy, 0), ext.at[lo:hi, 1:9, row : row + 1], ext.at[lo:hi, 1:9, to : to + 1]))
        for o in sorted(offsets, key=lambda o: -abs(o[1])):
            dx, dy, dz = o
            (a, b), (c, d) = rows_sent(dy, False)
            if dz:
                side = 0 if dz > 0 else 1
                found.append((o, pk.at[:, a:b], zb.at[side, 1 - dx, :, c:d]))
            elif dx:
                chans = slice(*(X_LOW if dx > 0 else X_HIGH))
                p_from, p_to = (8, 0) if dx > 0 else (1, 9)
                found.append((o, ext.at[chans, p_from, a:b], ext.at[chans, p_to, c:d]))
        return found

    def messages_rest():
        found = []
        for lo, hi in REST_LOW:
            found.append(((0, 1, 0), ext.at[lo:hi, 1:9, 23:24], ext.at[lo:hi, 1:9, 7:8]))
        for lo, hi in REST_HIGH:
            found.append(((0, -1, 0), ext.at[lo:hi, 1:9, 8:9], ext.at[lo:hi, 1:9, 24:25]))
        return found

    def messages_x(n, wide):
        x = xs.at[n, 1]
        found = []
        for o in offsets:
            dx, dy, dz = o
            if wide and dy:
                continue
            (a, b), (c, d) = rows_sent(dy, wide)
            if dz:
                side = 0 if dz > 0 else 1
                found.append((o, px.at[n, a:b], zx.at[n, side, 1 - dx, c:d]))
            elif dx:
                p_from, p_to = (8, 0) if dx > 0 else (1, 9)
                found.append((o, x.at[p_from, a:b], x.at[p_to, c:d]))
            else:
                found.append((o, x.at[1:9, a:b], x.at[1:9, c:d]))
        return found

    def exchange(found, send, recv):
        found = [
            (
                o,
                pltpu.make_async_remote_copy(
                    src_ref=a,
                    dst_ref=b,
                    send_sem=send.at[i],
                    recv_sem=recv.at[i],
                    device_id=device(o),
                    device_id_type=MESH,
                ),
            )
            for i, (o, a, b) in enumerate(found)
        ]

        def start():
            for o, c in found:
                pl.when(present(o))(c.start)

        def arrived():
            for o, c in found:
                pl.when(present(minus(o)))(c.wait_recv)

        def left():
            for o, c in found:
                pl.when(present(o))(c.wait_send)

        return start, arrived, left

    state = exchange(messages_state(), s_state, r_state)
    rest = exchange(messages_rest(), s_rest, r_rest)
    state[0]()
    rest[0]()

    tables = [[[t[c, k] for k in range(8)] for c in range(3)] for t in (b_tab, c_tab, v_tab)]

    def properties(p, sw, sg, m, r):
        b2 = r >= 4.0
        r = jnp.where(b2, r - 4.0, r)
        b1 = r >= 2.0
        b0 = jnp.where(b1, r - 2.0, r) >= 1.0

        def look(t):
            low = jnp.where(b1, jnp.where(b0, t[3], t[2]), jnp.where(b0, t[1], t[0]))
            high = jnp.where(b1, jnp.where(b0, t[7], t[6]), jnp.where(b0, t[5], t[4]))
            return jnp.where(b2, high, low)

        sat = (sw, 1.0 - sw - sg, sg)
        mob, slope, fac = [], [], []
        stored = None
        for c in range(3):
            rate = look(tables[1][c])
            f = look(tables[0][c]) * jnp.exp(rate * (p - 0.5))
            half = 0.5 * look(tables[2][c]) * f * sat[c] * sat[c]
            fac.append(f)
            mob.append(half)
            slope.append(rate * half)
            stored = rate * sat[c] if stored is None else stored + rate * sat[c]
        return [p, m, *mob, *slope], fac, sat, stored

    def across(plane, row):
        return (slice(plane, plane + 8), row)

    def weights(m, vol, old, fac, sat, stored):
        scale = 1.0 / jnp.where(m > 0, vol * stored, 1.0)
        return [scale / f for f in fac], [vol * f * v - o for f, v, o in zip(fac, sat, old)]

    STATE = (PR, SW, SG, AM, RG)

    def fill_own(i, carry):
        at = (i + 1, slice(8, 24))
        fields, fac, sat, stored = properties(*[ext[(ch, *at)] for ch in STATE])
        for f in range(8):
            fld[(1, f, *at)] = fields[f]
        old = [ext[(OM + c, *at)] for c in range(3)]
        ws, bs = weights(fields[1], ext[(PV, *at)], old, fac, sat, stored)
        for c in range(3):
            wts[c, i, 8:24] = ws[c]
            base[c, i, 8:24] = bs[c]
        return carry

    lax.fori_loop(0, 8, fill_own, 0)

    state[1]()

    shell = {}
    for row in (6, 7, 24, 25):
        at = across(1, row)
        shell[row] = properties(*[ext[(ch, *at)] for ch in STATE])
        for f in range(8):
            fld[(1, f, *at)] = shell[row][0][f]

    def fill_plane(plane):
        at = (plane, slice(6, 30))
        for f, value in enumerate(properties(*[ext[(ch, *at)] for ch in STATE])[0]):
            fld[(1, f, *at)] = value

    fill_plane(0)
    fill_plane(9)

    def gather(low, high):
        return jnp.where(even24, pltpu.roll(high, 127, 1), pltpu.roll(low, 1, 1))

    def spread(parts, start):
        before = pltpu.roll(parts[0], (128 - start - 14) % 128, 1)
        here = pltpu.roll(parts[1], (128 + 2 - start) % 128, 1)
        after = pltpu.roll(parts[2], (128 + 18 - start) % 128, 1)
        return jnp.where(lane24 < 2, before, jnp.where(lane24 < 18, here, after))

    parts = [[gather(zb[0, d, k, 6:30], zb[1, d, k, 6:30]) for d in range(3)] for k in range(2)]
    columns = [spread(parts[s // 8], 16 * (s % 8)) for s in range(5)]
    for f, value in enumerate(properties(*columns)[0]):
        zf[f, 6:30] = value
    for s in range(5, len(PACKED)):
        zf[3 + s, 6:30] = spread(parts[s // 8], 16 * (s % 8))

    def shift(i, carry):
        for f in range(8):
            value = fld[1, f, i, 6:30]
            edge = pltpu.roll(zf[f, 6:30], 127 - 2 * i, 1)
            fld[0, f, i, 6:30] = jnp.where(lane24 == 0, edge, pltpu.roll(value, 1, 1))
            fld[2, f, i, 6:30] = jnp.where(lane24 == 127, edge, pltpu.roll(value, 127, 1))
        for n, k in enumerate(T_ROLLED):
            at = {0: slice(6, 30), 1: slice(0, 24), -1: slice(8, 32)}[upper[k][1]]
            value = ext[TCH[k], i, at]
            edge = pltpu.roll(zf[8 + n, at], 127 - 2 * i, 1)
            if upper[k][2] > 0:
                tl[n, i, at] = jnp.where(lane24 == 0, edge, pltpu.roll(value, 1, 1))
            else:
                tl[n, i, at] = jnp.where(lane24 == 127, edge, pltpu.roll(value, 127, 1))
        return carry

    lax.fori_loop(0, 10, shift, 0)

    def equations(get, put, w, bs):
        centre = [get("fld", (1, f), 0, 0) for f in range(8)]
        p, m, mob, slope = centre[0], centre[1], centre[2:5], centre[5:8]
        mob_w = w[0] * mob[0] + w[1] * mob[1] + w[2] * mob[2]
        slope_w = w[0] * slope[0] + w[1] * slope[1] + w[2] * slope[2]
        zeros = jnp.zeros((8, 128), F32)
        sum_q, sum_t, sum_m = zeros, zeros, zeros
        sum_l = [zeros, zeros, zeros]
        for n, o in enumerate(offsets):
            dx, dy, dz = o
            if o in upper:
                t = get("ext", (TCH[upper.index(o)],), 0, 0)
            else:
                k = upper.index(minus(o))
                if dz:
                    t = get("tl", (T_ROLLED.index(k),), dx, dy)
                else:
                    t = get("ext", (TCH[k],), dx, dy)
            near = [get("fld", (dz + 1, f), dx, dy) for f in range(8)]
            t = t * near[1]
            q = t * (p - near[0])
            mw = w[0] * near[2] + w[1] * near[3] + w[2] * near[4]
            gw = w[0] * near[5] + w[1] * near[6] + w[2] * near[7]
            sum_q = sum_q + q
            sum_t = sum_t + t
            sum_m = sum_m + t * mw
            for c in range(3):
                sum_l[c] = sum_l[c] + q * near[2 + c]
            put("acoef", (n,), q * gw - t * (mob_w + mw))
        d = 1.0 + slope_w * sum_q + mob_w * sum_t + sum_m
        h = zeros
        for c in range(3):
            res = m * (bs[c] + mob[c] * sum_q + sum_l[c])
            put("resv", (c,), res)
            h = h - w[c] * res
        inv = jnp.where(m > 0, relax_weight / d, 0.0)
        put("dinv", (), inv)
        put("x0", (), inv * h)

    def assemble(i, carry):
        for a in (8, 16):
            refs = {"fld": fld, "ext": ext, "tl": tl}

            def get(name, lead, dx, dy, a=a, refs=refs):
                return refs[name][(*lead, i + 1 + dx, slice(a + dy, a + dy + 8))]

            def put(name, lead, value, a=a):
                at = slice(a, a + 8)
                if name == "x0":
                    xs[0, 1, i + 1, at] = value
                elif name == "resv":
                    res_out[lead[0], i, a - 8 : a] = value
                else:
                    {"acoef": acoef, "dinv": dinv}[name][(*lead, i, at)] = value

            at = (i, slice(a, a + 8))
            equations(get, put, [wts[(c, *at)] for c in range(3)], [base[(c, *at)] for c in range(3)])
        return carry

    lax.fori_loop(0, 8, assemble, 0)

    rest[1]()

    for row in (7, 24):
        refs = {"fld": fld, "ext": ext, "tl": tl}

        def get(name, lead, dx, dy, row=row, refs=refs):
            return refs[name][(*lead, *across(1 + dx, row + dy))]

        def put(name, lead, value, row=row):
            if name == "x0":
                xs[(0, 1, *across(1, row))] = value
            elif name != "resv":
                {"acoef": acoef, "dinv": dinv}[name][(*lead, *across(0, row))] = value

        fields, fac, sat, stored = shell[row]
        old = [get("ext", (OM + c,), 0, 0) for c in range(3)]
        equations(get, put, *weights(fields[1], get("ext", (PV,), 0, 0), old, fac, sat, stored))

    pending = []
    for n in range(3):
        wide = n != 1
        lo, hi = (7, 31) if wide else (8, 24)

        acc = jnp.zeros((hi - lo, 128), F32)
        pair = lane24[: hi - lo] // 2
        for x in range(8):
            acc = jnp.where(pair == x, pltpu.roll(xs[n, 1, x + 1, lo:hi], 2 * x + 1, 1), acc)
        px[n, lo:hi] = acc
        start, arrived, left = exchange(messages_x(n, wide), s_x.at[n], r_x.at[n])
        start()
        arrived()
        pending.append(left)
        column = spread([gather(zx[n, 0, d, 6:30], zx[n, 1, d, 6:30]) for d in range(3)], 0)

        for i in range(10):
            value = xs[n, 1, i, 6:30]
            edge = pltpu.roll(column, 127 - 2 * i, 1)
            xs[n, 0, i, 6:30] = jnp.where(lane24 == 0, edge, pltpu.roll(value, 1, 1))
            xs[n, 2, i, 6:30] = jnp.where(lane24 == 127, edge, pltpu.roll(value, 127, 1))

        def relaxed(near, coef, inv, start, value):
            total = jnp.zeros((8, 128), F32)
            for k, o in enumerate(offsets):
                total = total + coef(k) * near(*o)
            return start + (1.0 - relax_weight) * value - inv * total

        def sweep(i, carry, n=n, relaxed=relaxed):
            for a in (8, 16):
                at = slice(a, a + 8)
                value = relaxed(
                    lambda dx, dy, dz: xs[n, dz + 1, i + 1 + dx, a + dy : a + dy + 8],
                    lambda k: acoef[k, i, at],
                    dinv[i, at],
                    xs[0, 1, i + 1, at],
                    xs[n, 1, i + 1, at],
                )
                if n == 2:
                    x_out[i, a - 8 : a] = value
                else:
                    xs[n + 1, 1, i + 1, at] = value
            return carry

        lax.fori_loop(0, 8, sweep, 0)
        if n == 1:
            for row in (7, 24):
                xs[(2, 1, *across(1, row))] = relaxed(
                    lambda dx, dy, dz: xs[(1, dz + 1, *across(1 + dx, row + dy))],
                    lambda k: acoef[(k, *across(0, row))],
                    dinv[across(0, row)],
                    xs[(0, 1, *across(1, row))],
                    xs[(1, 1, *across(1, row))],
                )

    state[2]()
    rest[2]()
    for left in pending:
        left()


def body(cs, om, pv, tr, am, rg, b_tab, c_tab, v_tab):
    anywhere = pl.BlockSpec(memory_space=pltpu.HBM)
    vmem = lambda *s: pltpu.VMEM(s, F32)
    dma = lambda *s: pltpu.SemaphoreType.DMA(s)
    return pl.pallas_call(
        kernel,
        out_shape=(
            jax.ShapeDtypeStruct((3, 8, 16, 128), F32),
            jax.ShapeDtypeStruct((8, 16, 128), F32),
        ),
        in_specs=[anywhere] * 9,
        out_specs=(pl.BlockSpec(memory_space=pltpu.VMEM),) * 2,
        scratch_shapes=[
            *[pltpu.SMEM((3, 8), F32)] * 3,
            vmem(NCH, NP, NR, 128),
            pltpu.VMEM((2, 8, 16, 128), jnp.int32),
            vmem(3, 8, NP, NR, 128),
            vmem(len(T_ROLLED), NP, NR, 128),
            vmem(3, 8, NR, 128),
            vmem(3, 8, NR, 128),
            vmem(26, 8, NR, 128),
            vmem(8, NR, 128),
            vmem(3, 3, NP, NR, 128),
            vmem(3, NR, 128),
            vmem(3, 2, 3, NR, 128),
            vmem(2, NR, 128),
            vmem(2, 3, 2, NR, 128),
            vmem(8 + len(T_ROLLED), NR, 128),
            dma(12),
            dma(28),
            dma(28),
            dma(3),
            dma(3),
            dma(3, 26),
            dma(3, 26),
        ],
        compiler_params=pltpu.CompilerParams(
            collective_id=0, has_side_effects=True, vmem_limit_bytes=60 * 1024 * 1024
        ),
    )(cs, om, pv, tr, am, rg, b_tab, c_tab, v_tab)


def solution(mesh):
    four = P(None, "gx", "gy", "gz")
    three = P("gx", "gy", "gz")
    return jax.shard_map(
        body,
        mesh=mesh,
        in_specs=(four, four, three, four, three, three, P(), P(), P()),
        out_specs=(four, three),
        check_vma=False,
    )
```

```python
import functools
import itertools

import jax
import jax.numpy as jnp
from jax import lax
from jax.experimental import pallas as pl
from jax.experimental.pallas import tpu as pltpu
from jax.sharding import PartitionSpec as P

MESH = pl.DeviceIdType.MESH
F32 = jnp.float32
AXES = ("gx", "gy", "gz")
relax_weight = 0.7

offsets = [o for o in itertools.product((-1, 0, 1), repeat=3) if o != (0, 0, 0)]
upper = [o for o in offsets if o > (0, 0, 0)]
minus = lambda o: (-o[0], -o[1], -o[2])

OM, PV, PR, SW, SG, AM, RG = 0, 3, 11, 12, 13, 14, 15
TCH = {4: 4, 5: 5, 6: 6, 7: 7, 8: 8, 9: 9, 0: 10, 10: 16, 11: 17, 12: 18, 1: 19, 2: 20, 3: 21}
NCH = 22
X_LOW, X_HIGH = (4, 19), (11, 16)
Y_LOW, Y_LOW2, Y_HIGH = (7, 22), (11, 22), (4, 16)
REST_LOW, REST_HIGH = ((0, 7),), ((0, 4), (16, 22))

NP, NR = 10, 32
T_ROLLED = [k for k, o in enumerate(upper) if o[2] != 0]
PACKED = [PR, SW, SG, AM, RG] + [TCH[k] for k in T_ROLLED]


def rows_sent(dy, wide):
    if dy == 0:
        return (7, 25) if wide else (8, 24), (7, 25) if wide else (8, 24)
    if dy > 0:
        return (22, 24), (6, 8)
    return (8, 10), (24, 26)


def kernel(
    cs, om, pv, tr, am, rg, b_hbm, c_hbm, v_hbm,
    res_out, x_out,
    b_tab, c_tab, v_tab, ext, ints, fld, tl, wts, base, acoef, dinv, xs, px, zx, pk, zb, zf, resv, xv,
    in_sem, out_sem, s_state, r_state, s_rest, r_rest, s_x, r_x,
):
    me = [lax.axis_index(a) for a in AXES]
    dims = [lax.axis_size(a) for a in AXES]

    def present(o):
        cond = None
        for i, s in enumerate(o):
            if s:
                here = me[i] + s >= 0 if s < 0 else me[i] + s < dims[i]
                cond = here if cond is None else cond & here
        return cond

    def device(o):
        return tuple(jnp.clip(me[i] + s, 0, dims[i] - 1) if s else me[i] for i, s in enumerate(o))

    loads = [
        (cs, ext.at[PR : PR + 3, 1:9, 8:24]),
        (om, ext.at[OM : OM + 3, 1:9, 8:24]),
        (pv, ext.at[PV, 1:9, 8:24]),
        (am, ints.at[0]),
        (rg, ints.at[1]),
        (tr.at[0], ext.at[10, 1:9, 8:24]),
        (tr.at[4:10], ext.at[4:10, 1:9, 8:24]),
        (tr.at[10:13], ext.at[16:19, 1:9, 8:24]),
        (tr.at[1:4], ext.at[19:22, 1:9, 8:24]),
        (b_hbm, b_tab),
        (c_hbm, c_tab),
        (v_hbm, v_tab),
    ]
    copies = [pltpu.make_async_copy(a, b, in_sem.at[i]) for i, (a, b) in enumerate(loads)]
    for c in copies:
        c.start()

    first = [me[i] == 0 for i in range(3)]
    last = [me[i] == dims[i] - 1 for i in range(3)]

    def zero(ref):
        ref[...] = jnp.zeros(ref.shape, ref.dtype)

    @pl.when(first[0])
    def _():
        zero(ext.at[4:19, 0])

    @pl.when(last[0])
    def _():
        zero(ext.at[11:16, 9])

    @pl.when(first[1])
    def _():
        zero(ext.at[:, :, 0:8])

    @pl.when(last[1])
    def _():
        zero(ext.at[:, :, 24:32])

    border = first[0] | first[1] | first[2] | last[0] | last[1] | last[2]

    @pl.when(border)
    def _():
        zero(zb)
        zero(zx)
        for n in range(3):
            zero(xs.at[n, 1])

    barrier = pltpu.get_barrier_semaphore()
    for o in offsets:

        @pl.when(present(o))
        def _(o=o):
            pl.semaphore_signal(barrier, inc=1, device_id=device(o), device_id_type=MESH)

    for c in copies:
        c.wait()

    def convert(i, carry):
        ext[AM, i + 1, 8:24] = ints[0, i].astype(F32)
        ext[RG, i + 1, 8:24] = ints[1, i].astype(F32)
        return carry

    lax.fori_loop(0, 8, convert, 0)

    peers = 1
    for i in range(3):
        peers = peers * (1 + (me[i] > 0).astype(jnp.int32) + (me[i] < dims[i] - 1).astype(jnp.int32))
    pl.semaphore_wait(barrier, peers - 1)

    def messages_state():
        found = []
        for dy, (lo, hi), row, to in (
            (1, Y_LOW, 23, 7),
            (-1, Y_HIGH, 8, 24),
            (1, Y_LOW2, 22, 6),
            (-1, Y_HIGH, 9, 25),
        ):
            found.append(((0, dy, 0), ext.at[lo:hi, 1:9, row : row + 1], ext.at[lo:hi, 1:9, to : to + 1]))
        for o in sorted(offsets, key=lambda o: -abs(o[1])):
            dx, dy, dz = o
            (a, b), (c, d) = rows_sent(dy, False)
            if dz:
                side = 0 if dz > 0 else 1
                found.append((o, pk.at[:, a:b], zb.at[side, 1 - dx, :, c:d]))
            elif dx:
                chans = slice(*(X_LOW if dx > 0 else X_HIGH))
                p_from, p_to = (8, 0) if dx > 0 else (1, 9)
                found.append((o, ext.at[chans, p_from, a:b], ext.at[chans, p_to, c:d]))
        return found

    def messages_rest():
        found = []
        for lo, hi in REST_LOW:
            found.append(((0, 1, 0), ext.at[lo:hi, 1:9, 23:24], ext.at[lo:hi, 1:9, 7:8]))
        for lo, hi in REST_HIGH:
            found.append(((0, -1, 0), ext.at[lo:hi, 1:9, 8:9], ext.at[lo:hi, 1:9, 24:25]))
        return found

    def messages_x(n, wide):
        x = xs.at[n, 1]
        found = []
        for o in sorted(offsets, key=lambda o: (-abs(o[1]), -abs(o[0]) - abs(o[2]))):
            dx, dy, dz = o
            if wide and dy:
                continue
            (a, b), (c, d) = rows_sent(dy, wide)
            if dz:
                side = 0 if dz > 0 else 1
                found.append((o, px.at[n, a:b], zx.at[n, side, 1 - dx, c:d]))
            elif dx:
                p_from, p_to = (8, 0) if dx > 0 else (1, 9)
                found.append((o, x.at[p_from, a:b], x.at[p_to, c:d]))
            else:
                found.append((o, x.at[1:9, a:b], x.at[1:9, c:d]))
        return found

    def exchange(found, send, recv):
        found = [
            (
                o,
                pltpu.make_async_remote_copy(
                    src_ref=a,
                    dst_ref=b,
                    send_sem=send.at[i],
                    recv_sem=recv.at[i],
                    device_id=device(o),
                    device_id_type=MESH,
                ),
            )
            for i, (o, a, b) in enumerate(found)
        ]

        def start(along_z=None):
            for o, c in found:
                if along_z is None or along_z == (o[2] != 0):
                    pl.when(present(o))(c.start)

        def arrived():
            for o, c in found:
                pl.when(present(minus(o)))(c.wait_recv)

        def left():
            for o, c in found:
                pl.when(present(o))(c.wait_send)

        return start, arrived, left

    state = exchange(messages_state(), s_state, r_state)
    rest = exchange(messages_rest(), s_rest, r_rest)
    state[0](False)
    lane16 = lax.broadcasted_iota(jnp.int32, (16, 128), 1)
    lane24 = lax.broadcasted_iota(jnp.int32, (24, 128), 1)
    even24 = lane24 % 2 == 0

    def pack(x, accs):
        accs = list(accs)
        for s, ch in enumerate(PACKED):
            to = 16 * (s % 8) + 2 * x
            moved = pltpu.roll(ext[ch, x + 1, 8:24], to + 1, 1)
            accs[s // 8] = jnp.where((lane16 == to) | (lane16 == to + 1), moved, accs[s // 8])
        return tuple(accs)

    packed = lax.fori_loop(0, 8, pack, (jnp.zeros((16, 128), F32),) * 2, unroll=2)
    for k in range(2):
        pk[k, 8:24] = packed[k]

    state[0](True)
    rest[0]()

    tables = [[[t[c, k] for k in range(8)] for c in range(3)] for t in (b_tab, c_tab, v_tab)]

    def properties(p, sw, sg, m, r):
        b2 = r >= 4.0
        r = jnp.where(b2, r - 4.0, r)
        b1 = r >= 2.0
        b0 = jnp.where(b1, r - 2.0, r) >= 1.0

        def look(t):
            low = jnp.where(b1, jnp.where(b0, t[3], t[2]), jnp.where(b0, t[1], t[0]))
            high = jnp.where(b1, jnp.where(b0, t[7], t[6]), jnp.where(b0, t[5], t[4]))
            return jnp.where(b2, high, low)

        sat = (sw, 1.0 - sw - sg, sg)
        mob, slope, fac = [], [], []
        stored = None
        for c in range(3):
            rate = look(tables[1][c])
            f = look(tables[0][c]) * jnp.exp(rate * (p - 0.5))
            half = 0.5 * look(tables[2][c]) * f * sat[c] * sat[c]
            fac.append(f)
            mob.append(half)
            slope.append(rate * half)
            stored = rate * sat[c] if stored is None else stored + rate * sat[c]
        return [p, m, *mob, *slope], fac, sat, stored

    def across(plane, row):
        return (slice(plane, plane + 8), row)

    flat = lambda ref, n: ref.reshape(*ref.shape[:-3], n * NR, 128)
    fld_f, tl_f, acoef_f, dinv_f = flat(fld, NP), flat(tl, NP), flat(acoef, 8), flat(dinv, 8)

    def strided(plane, row):
        return (pl.ds(plane * NR + row, 8, stride=NR), slice(None))

    def weights(m, vol, old, fac, sat, stored):
        scale = 1.0 / jnp.where(m > 0, vol * stored, 1.0)
        return [scale / f for f in fac], [vol * f * v - o for f, v, o in zip(fac, sat, old)]

    STATE = (PR, SW, SG, AM, RG)

    def fill_own(i, carry):
        at = (i + 1, slice(8, 24))
        fields, fac, sat, stored = properties(*[ext[(ch, *at)] for ch in STATE])
        for f in range(8):
            fld[(1, f, *at)] = fields[f]
        old = [ext[(OM + c, *at)] for c in range(3)]
        ws, bs = weights(fields[1], ext[(PV, *at)], old, fac, sat, stored)
        for c in range(3):
            wts[c, i, 8:24] = ws[c]
            base[c, i, 8:24] = bs[c]
        return carry

    lax.fori_loop(0, 8, fill_own, 0)

    state[1]()

    shell = {}
    for row in (6, 7, 24, 25):
        at = across(1, row)
        shell[row] = properties(*[ext[(ch, *at)] for ch in STATE])
        for f in range(8):
            fld_f[(1, f, *strided(1, row))] = shell[row][0][f]

    def fill_plane(plane):
        at = (plane, slice(6, 30))
        for f, value in enumerate(properties(*[ext[(ch, *at)] for ch in STATE])[0]):
            fld[(1, f, *at)] = value

    fill_plane(0)
    fill_plane(9)

    def gather(low, high):
        return jnp.where(even24, pltpu.roll(high, 127, 1), pltpu.roll(low, 1, 1))

    def spread(parts, start):
        before = pltpu.roll(parts[0], (128 - start - 14) % 128, 1)
        here = pltpu.roll(parts[1], (128 + 2 - start) % 128, 1)
        after = pltpu.roll(parts[2], (128 + 18 - start) % 128, 1)
        return jnp.where(lane24 < 2, before, jnp.where(lane24 < 18, here, after))

    parts = [[gather(zb[0, d, k, 6:30], zb[1, d, k, 6:30]) for d in range(3)] for k in range(2)]
    columns = [spread(parts[s // 8], 16 * (s % 8)) for s in range(5)]
    for f, value in enumerate(properties(*columns)[0]):
        zf[f, 6:30] = value
    for s in range(5, len(PACKED)):
        zf[3 + s, 6:30] = spread(parts[s // 8], 16 * (s % 8))

    def shift(i, carry):
        for f in range(8):
            value = fld[1, f, i, 6:30]
            edge = pltpu.roll(zf[f, 6:30], 127 - 2 * i, 1)
            fld[0, f, i, 6:30] = jnp.where(lane24 == 0, edge, pltpu.roll(value, 1, 1))
            fld[2, f, i, 6:30] = jnp.where(lane24 == 127, edge, pltpu.roll(value, 127, 1))
        for n, k in enumerate(T_ROLLED):
            at = {0: slice(6, 30), 1: slice(0, 24), -1: slice(8, 32)}[upper[k][1]]
            value = ext[TCH[k], i, at]
            edge = pltpu.roll(zf[8 + n, at], 127 - 2 * i, 1)
            if upper[k][2] > 0:
                tl[n, i, at] = jnp.where(lane24 == 0, edge, pltpu.roll(value, 1, 1))
            else:
                tl[n, i, at] = jnp.where(lane24 == 127, edge, pltpu.roll(value, 127, 1))
        return carry

    lax.fori_loop(0, 10, shift, 0, unroll=2)

    def equations(get, put, w, bs):
        centre = [get("fld", (1, f), 0, 0) for f in range(8)]
        p, m, mob, slope = centre[0], centre[1], centre[2:5], centre[5:8]
        mob_w = w[0] * mob[0] + w[1] * mob[1] + w[2] * mob[2]
        slope_w = w[0] * slope[0] + w[1] * slope[1] + w[2] * slope[2]
        zeros = jnp.zeros((8, 128), F32)
        sum_q, sum_t, sum_m = zeros, zeros, zeros
        sum_l = [zeros, zeros, zeros]
        for n, o in enumerate(offsets):
            dx, dy, dz = o
            if o in upper:
                t = get("ext", (TCH[upper.index(o)],), 0, 0)
            else:
                k = upper.index(minus(o))
                if dz:
                    t = get("tl", (T_ROLLED.index(k),), dx, dy)
                else:
                    t = get("ext", (TCH[k],), dx, dy)
            near = [get("fld", (dz + 1, f), dx, dy) for f in range(8)]
            t = t * near[1]
            q = t * (p - near[0])
            mw = w[0] * near[2] + w[1] * near[3] + w[2] * near[4]
            gw = w[0] * near[5] + w[1] * near[6] + w[2] * near[7]
            sum_q = sum_q + q
            sum_t = sum_t + t
            sum_m = sum_m + t * mw
            for c in range(3):
                sum_l[c] = sum_l[c] + q * near[2 + c]
            put("acoef", (n,), q * gw - t * (mob_w + mw))
        d = 1.0 + slope_w * sum_q + mob_w * sum_t + sum_m
        h = zeros
        for c in range(3):
            res = m * (bs[c] + mob[c] * sum_q + sum_l[c])
            put("resv", (c,), res)
            h = h - w[c] * res
        inv = jnp.where(m > 0, relax_weight / d, 0.0)
        put("dinv", (), inv)
        put("x0", (), inv * h)

    def assemble(i, carry):
        for a in (8, 16):
            refs = {"fld": fld, "ext": ext, "tl": tl}

            def get(name, lead, dx, dy, a=a, refs=refs):
                return refs[name][(*lead, i + 1 + dx, slice(a + dy, a + dy + 8))]

            def put(name, lead, value, a=a):
                at = slice(a, a + 8)
                if name == "x0":
                    xs[0, 1, i + 1, at] = value
                elif name == "resv":
                    resv[lead[0], i, a - 8 : a] = value
                else:
                    {"acoef": acoef, "dinv": dinv}[name][(*lead, i, at)] = value

            at = (i, slice(a, a + 8))
            equations(get, put, [wts[(c, *at)] for c in range(3)], [base[(c, *at)] for c in range(3)])
        return carry

    lax.fori_loop(0, 8, assemble, 0)
    out_copies = [pltpu.make_async_copy(resv, res_out, out_sem.at[0]), pltpu.make_async_copy(xv, x_out, out_sem.at[1])]
    out_copies[0].start()

    rest[1]()

    for row in (7, 24):
        def get(name, lead, dx, dy, row=row):
            if name == "ext":
                return ext[(*lead, *across(1 + dx, row + dy))]
            return {"fld": fld_f, "tl": tl_f}[name][(*lead, *strided(1 + dx, row + dy))]

        def put(name, lead, value, row=row):
            if name == "x0":
                xs[(0, 1, *across(1, row))] = value
            elif name != "resv":
                {"acoef": acoef_f, "dinv": dinv_f}[name][(*lead, *strided(0, row))] = value

        fields, fac, sat, stored = shell[row]
        old = [get("ext", (OM + c,), 0, 0) for c in range(3)]
        equations(get, put, *weights(fields[1], get("ext", (PV,), 0, 0), old, fac, sat, stored))

    pending = []
    for n in range(3):
        wide = n != 1
        lo, hi = (7, 31) if wide else (8, 24)

        acc = jnp.zeros((hi - lo, 128), F32)
        pair = lane24[: hi - lo] // 2
        for x in range(8):
            acc = jnp.where(pair == x, pltpu.roll(xs[n, 1, x + 1, lo:hi], 2 * x + 1, 1), acc)
        px[n, lo:hi] = acc
        start, arrived, left = exchange(messages_x(n, wide), s_x.at[n], r_x.at[n])
        start()
        arrived()
        pending.append(left)
        column = spread([gather(zx[n, 0, d, 6:30], zx[n, 1, d, 6:30]) for d in range(3)], 0)

        for i in range(10):
            value = xs[n, 1, i, 6:30]
            edge = pltpu.roll(column, 127 - 2 * i, 1)
            xs[n, 0, i, 6:30] = jnp.where(lane24 == 0, edge, pltpu.roll(value, 1, 1))
            xs[n, 2, i, 6:30] = jnp.where(lane24 == 127, edge, pltpu.roll(value, 127, 1))

        def relaxed(near, coef, inv, start, value):
            total = jnp.zeros((8, 128), F32)
            for k, o in enumerate(offsets):
                total = total + coef(k) * near(*o)
            return start + (1.0 - relax_weight) * value - inv * total

        def sweep(i, carry, n=n, relaxed=relaxed):
            for a in (8, 16):
                at = slice(a, a + 8)
                value = relaxed(
                    lambda dx, dy, dz: xs[n, dz + 1, i + 1 + dx, a + dy : a + dy + 8],
                    lambda k: acoef[k, i, at],
                    dinv[i, at],
                    xs[0, 1, i + 1, at],
                    xs[n, 1, i + 1, at],
                )
                if n == 2:
                    xv[i, a - 8 : a] = value
                else:
                    xs[n + 1, 1, i + 1, at] = value
            return carry

        lax.fori_loop(0, 8, sweep, 0, unroll=4)
        if n == 1:
            for row in (7, 24):
                xs[(2, 1, *across(1, row))] = relaxed(
                    lambda dx, dy, dz: xs[(1, dz + 1, *across(1 + dx, row + dy))],
                    lambda k: acoef_f[(k, *strided(0, row))],
                    dinv_f[strided(0, row)],
                    xs[(0, 1, *across(1, row))],
                    xs[(1, 1, *across(1, row))],
                )

    out_copies[1].start()
    state[2]()
    rest[2]()
    for left in pending:
        left()
    for c in out_copies:
        c.wait()


def body(cs, om, pv, tr, am, rg, b_tab, c_tab, v_tab):
    anywhere = pl.BlockSpec(memory_space=pltpu.HBM)
    vmem = lambda *s: pltpu.VMEM(s, F32)
    dma = lambda *s: pltpu.SemaphoreType.DMA(s)
    return pl.pallas_call(
        kernel,
        out_shape=(
            jax.ShapeDtypeStruct((3, 8, 16, 128), F32),
            jax.ShapeDtypeStruct((8, 16, 128), F32),
        ),
        in_specs=[anywhere] * 9,
        out_specs=(anywhere,) * 2,
        scratch_shapes=[
            *[pltpu.SMEM((3, 8), F32)] * 3,
            vmem(NCH, NP, NR, 128),
            pltpu.VMEM((2, 8, 16, 128), jnp.int32),
            vmem(3, 8, NP, NR, 128),
            vmem(len(T_ROLLED), NP, NR, 128),
            vmem(3, 8, NR, 128),
            vmem(3, 8, NR, 128),
            vmem(26, 8, NR, 128),
            vmem(8, NR, 128),
            vmem(3, 3, NP, NR, 128),
            vmem(3, NR, 128),
            vmem(3, 2, 3, NR, 128),
            vmem(2, NR, 128),
            vmem(2, 3, 2, NR, 128),
            vmem(8 + len(T_ROLLED), NR, 128),
            vmem(3, 8, 16, 128),
            vmem(8, 16, 128),
            dma(12),
            dma(2),
            dma(28),
            dma(28),
            dma(3),
            dma(3),
            dma(3, 26),
            dma(3, 26),
        ],
        compiler_params=pltpu.CompilerParams(
            collective_id=0, has_side_effects=True, vmem_limit_bytes=60 * 1024 * 1024
        ),
    )(cs, om, pv, tr, am, rg, b_tab, c_tab, v_tab)


def solution(mesh):
    four = P(None, "gx", "gy", "gz")
    three = P("gx", "gy", "gz")
    return jax.shard_map(
        body,
        mesh=mesh,
        in_specs=(four, four, three, four, three, three, P(), P(), P()),
        out_specs=(four, three),
        check_vma=False,
    )
```

```python
import functools
import itertools

import jax
import jax.numpy as jnp
from jax import lax
from jax.experimental import pallas as pl
from jax.experimental.pallas import tpu as pltpu
from jax.sharding import PartitionSpec as P

MESH = pl.DeviceIdType.MESH
F32 = jnp.float32
AXES = ("gx", "gy", "gz")
relax_weight = 0.7

offsets = [o for o in itertools.product((-1, 0, 1), repeat=3) if o != (0, 0, 0)]
upper = [o for o in offsets if o > (0, 0, 0)]
minus = lambda o: (-o[0], -o[1], -o[2])

OM, PV, PR, SW, SG, AM, RG = 0, 3, 11, 12, 13, 14, 15
TCH = {4: 4, 5: 5, 6: 6, 7: 7, 8: 8, 9: 9, 0: 10, 10: 16, 11: 17, 12: 18, 1: 19, 2: 20, 3: 21}
NCH = 22
X_LOW, X_HIGH = (4, 19), (11, 16)
Y_LOW, Y_LOW2, Y_HIGH = (7, 22), (11, 22), (4, 16)
REST_LOW, REST_HIGH = ((0, 7),), ((0, 4), (16, 22))

NP, NR = 10, 32
T_ROLLED = [k for k, o in enumerate(upper) if o[2] != 0]
PACKED = [PR, SW, SG, AM, RG] + [TCH[k] for k in T_ROLLED]


def rows_sent(dy, wide):
    if dy == 0:
        return (7, 25) if wide else (8, 24), (7, 25) if wide else (8, 24)
    if dy > 0:
        return (22, 24), (6, 8)
    return (8, 10), (24, 26)


def kernel(
    cs, om, pv, tr, am, rg, b_hbm, c_hbm, v_hbm,
    res_out, x_out,
    b_tab, c_tab, v_tab, ext, ints, fld, tl, wts, base, acoef, dinv, xs, px, zx, pk, zb, zf, resv, xv,
    in_sem, out_sem, s_state, r_state, s_rest, r_rest, s_x, r_x,
):
    me = [lax.axis_index(a) for a in AXES]
    dims = [lax.axis_size(a) for a in AXES]

    def present(o):
        cond = None
        for i, s in enumerate(o):
            if s:
                here = me[i] + s >= 0 if s < 0 else me[i] + s < dims[i]
                cond = here if cond is None else cond & here
        return cond

    def device(o):
        return tuple(jnp.clip(me[i] + s, 0, dims[i] - 1) if s else me[i] for i, s in enumerate(o))

    loads = [
        (cs, ext.at[PR : PR + 3, 1:9, 8:24]),
        (om, ext.at[OM : OM + 3, 1:9, 8:24]),
        (pv, ext.at[PV, 1:9, 8:24]),
        (am, ints.at[0]),
        (rg, ints.at[1]),
        (tr.at[0], ext.at[10, 1:9, 8:24]),
        (tr.at[4:10], ext.at[4:10, 1:9, 8:24]),
        (tr.at[10:13], ext.at[16:19, 1:9, 8:24]),
        (tr.at[1:4], ext.at[19:22, 1:9, 8:24]),
        (b_hbm, b_tab),
        (c_hbm, c_tab),
        (v_hbm, v_tab),
    ]
    copies = [pltpu.make_async_copy(a, b, in_sem.at[i]) for i, (a, b) in enumerate(loads)]
    for c in copies:
        c.start()

    first = [me[i] == 0 for i in range(3)]
    last = [me[i] == dims[i] - 1 for i in range(3)]

    def zero(ref):
        ref[...] = jnp.zeros(ref.shape, ref.dtype)

    @pl.when(first[0])
    def _():
        zero(ext.at[4:19, 0])

    @pl.when(last[0])
    def _():
        zero(ext.at[11:16, 9])

    @pl.when(first[1])
    def _():
        zero(ext.at[:, :, 0:8])

    @pl.when(last[1])
    def _():
        zero(ext.at[:, :, 24:32])

    border = first[0] | first[1] | first[2] | last[0] | last[1] | last[2]

    @pl.when(border)
    def _():
        zero(zb)
        zero(zx)
        for n in range(3):
            zero(xs.at[n, 1])

    barrier = pltpu.get_barrier_semaphore()
    for o in offsets:

        @pl.when(present(o))
        def _(o=o):
            pl.semaphore_signal(barrier, inc=1, device_id=device(o), device_id_type=MESH)

    for c in copies:
        c.wait()

    def convert(i, carry):
        ext[AM, i + 1, 8:24] = ints[0, i].astype(F32)
        ext[RG, i + 1, 8:24] = ints[1, i].astype(F32)
        return carry

    lax.fori_loop(0, 8, convert, 0)

    peers = 1
    for i in range(3):
        peers = peers * (1 + (me[i] > 0).astype(jnp.int32) + (me[i] < dims[i] - 1).astype(jnp.int32))
    pl.semaphore_wait(barrier, peers - 1)

    def messages_state():
        found = []
        for dy, (lo, hi), row, to in (
            (1, Y_LOW, 23, 7),
            (-1, Y_HIGH, 8, 24),
            (1, Y_LOW2, 22, 6),
            (-1, Y_HIGH, 9, 25),
        ):
            found.append(((0, dy, 0), ext.at[lo:hi, 1:9, row : row + 1], ext.at[lo:hi, 1:9, to : to + 1]))
        for o in sorted(offsets, key=lambda o: -abs(o[1])):
            dx, dy, dz = o
            (a, b), (c, d) = rows_sent(dy, False)
            if dz:
                side = 0 if dz > 0 else 1
                found.append((o, pk.at[:, a:b], zb.at[side, 1 - dx, :, c:d]))
            elif dx:
                chans = slice(*(X_LOW if dx > 0 else X_HIGH))
                p_from, p_to = (8, 0) if dx > 0 else (1, 9)
                found.append((o, ext.at[chans, p_from, a:b], ext.at[chans, p_to, c:d]))
        return found

    def messages_rest():
        found = []
        for lo, hi in REST_LOW:
            found.append(((0, 1, 0), ext.at[lo:hi, 1:9, 23:24], ext.at[lo:hi, 1:9, 7:8]))
        for lo, hi in REST_HIGH:
            found.append(((0, -1, 0), ext.at[lo:hi, 1:9, 8:9], ext.at[lo:hi, 1:9, 24:25]))
        return found

    def messages_x(n, wide):
        x = xs.at[n, 1]
        found = []
        for o in sorted(offsets, key=lambda o: (-abs(o[1]), -abs(o[0]) - abs(o[2]))):
            dx, dy, dz = o
            if wide and dy:
                continue
            (a, b), (c, d) = rows_sent(dy, wide)
            if dz:
                side = 0 if dz > 0 else 1
                found.append((o, px.at[n, a:b], zx.at[n, side, 1 - dx, c:d]))
            elif dx:
                p_from, p_to = (8, 0) if dx > 0 else (1, 9)
                found.append((o, x.at[p_from, a:b], x.at[p_to, c:d]))
            else:
                found.append((o, x.at[1:9, a:b], x.at[1:9, c:d]))
        return found

    def exchange(found, send, recv):
        found = [
            (
                o,
                pltpu.make_async_remote_copy(
                    src_ref=a,
                    dst_ref=b,
                    send_sem=send.at[i],
                    recv_sem=recv.at[i],
                    device_id=device(o),
                    device_id_type=MESH,
                ),
            )
            for i, (o, a, b) in enumerate(found)
        ]

        def start(along_z=None):
            for o, c in found:
                if along_z is None or along_z == (o[2] != 0):
                    pl.when(present(o))(c.start)

        def arrived():
            for o, c in found:
                pl.when(present(minus(o)))(c.wait_recv)

        def left():
            for o, c in found:
                pl.when(present(o))(c.wait_send)

        return start, arrived, left

    state = exchange(messages_state(), s_state, r_state)
    rest = exchange(messages_rest(), s_rest, r_rest)
    state[0](False)
    lane16 = lax.broadcasted_iota(jnp.int32, (16, 128), 1)
    lane24 = lax.broadcasted_iota(jnp.int32, (24, 128), 1)
    even24 = lane24 % 2 == 0

    def pack(x, accs):
        accs = list(accs)
        for s, ch in enumerate(PACKED):
            to = 16 * (s % 8) + 2 * x
            moved = pltpu.roll(ext[ch, x + 1, 8:24], to + 1, 1)
            accs[s // 8] = jnp.where((lane16 == to) | (lane16 == to + 1), moved, accs[s // 8])
        return tuple(accs)

    packed = lax.fori_loop(0, 8, pack, (jnp.zeros((16, 128), F32),) * 2, unroll=4)
    for k in range(2):
        pk[k, 8:24] = packed[k]

    state[0](True)
    rest[0]()

    tables = [[[t[c, k] for k in range(8)] for c in range(3)] for t in (b_tab, c_tab, v_tab)]

    def properties(p, sw, sg, m, r):
        b2 = r >= 4.0
        r = jnp.where(b2, r - 4.0, r)
        b1 = r >= 2.0
        b0 = jnp.where(b1, r - 2.0, r) >= 1.0

        def look(t):
            low = jnp.where(b1, jnp.where(b0, t[3], t[2]), jnp.where(b0, t[1], t[0]))
            high = jnp.where(b1, jnp.where(b0, t[7], t[6]), jnp.where(b0, t[5], t[4]))
            return jnp.where(b2, high, low)

        sat = (sw, 1.0 - sw - sg, sg)
        mob, slope, fac = [], [], []
        stored = None
        for c in range(3):
            rate = look(tables[1][c])
            f = look(tables[0][c]) * jnp.exp(rate * (p - 0.5))
            half = 0.5 * look(tables[2][c]) * f * sat[c] * sat[c]
            fac.append(f)
            mob.append(half)
            slope.append(rate * half)
            stored = rate * sat[c] if stored is None else stored + rate * sat[c]
        return [p, m, *mob, *slope], fac, sat, stored

    def across(plane, row):
        return (slice(plane, plane + 8), row)

    flat = lambda ref, n: ref.reshape(*ref.shape[:-3], n * NR, 128)
    fld_f, tl_f, acoef_f, dinv_f = flat(fld, NP), flat(tl, NP), flat(acoef, 8), flat(dinv, 8)

    def strided(plane, row):
        return (pl.ds(plane * NR + row, 8, stride=NR), slice(None))

    def weights(m, vol, old, fac, sat, stored):
        scale = 1.0 / jnp.where(m > 0, vol * stored, 1.0)
        return [scale / f for f in fac], [vol * f * v - o for f, v, o in zip(fac, sat, old)]

    STATE = (PR, SW, SG, AM, RG)

    def fill_own(i, carry):
        at = (i + 1, slice(8, 24))
        fields, fac, sat, stored = properties(*[ext[(ch, *at)] for ch in STATE])
        for f in range(8):
            fld[(1, f, *at)] = fields[f]
        old = [ext[(OM + c, *at)] for c in range(3)]
        ws, bs = weights(fields[1], ext[(PV, *at)], old, fac, sat, stored)
        for c in range(3):
            wts[c, i, 8:24] = ws[c]
            base[c, i, 8:24] = bs[c]
        return carry

    lax.fori_loop(0, 8, fill_own, 0)

    state[1]()

    shell = {}
    for row in (6, 7, 24, 25):
        at = across(1, row)
        shell[row] = properties(*[ext[(ch, *at)] for ch in STATE])
        for f in range(8):
            fld_f[(1, f, *strided(1, row))] = shell[row][0][f]

    def fill_plane(plane):
        at = (plane, slice(6, 30))
        for f, value in enumerate(properties(*[ext[(ch, *at)] for ch in STATE])[0]):
            fld[(1, f, *at)] = value

    fill_plane(0)
    fill_plane(9)

    def gather(low, high):
        return jnp.where(even24, pltpu.roll(high, 127, 1), pltpu.roll(low, 1, 1))

    def spread(parts, start):
        before = pltpu.roll(parts[0], (128 - start - 14) % 128, 1)
        here = pltpu.roll(parts[1], (128 + 2 - start) % 128, 1)
        after = pltpu.roll(parts[2], (128 + 18 - start) % 128, 1)
        return jnp.where(lane24 < 2, before, jnp.where(lane24 < 18, here, after))

    parts = [[gather(zb[0, d, k, 6:30], zb[1, d, k, 6:30]) for d in range(3)] for k in range(2)]
    columns = [spread(parts[s // 8], 16 * (s % 8)) for s in range(5)]
    for f, value in enumerate(properties(*columns)[0]):
        zf[f, 6:30] = value
    for s in range(5, len(PACKED)):
        zf[3 + s, 6:30] = spread(parts[s // 8], 16 * (s % 8))

    def shift(i, carry):
        for f in range(8):
            value = fld[1, f, i, 6:30]
            edge = pltpu.roll(zf[f, 6:30], 127 - 2 * i, 1)
            fld[0, f, i, 6:30] = jnp.where(lane24 == 0, edge, pltpu.roll(value, 1, 1))
            fld[2, f, i, 6:30] = jnp.where(lane24 == 127, edge, pltpu.roll(value, 127, 1))
        for n, k in enumerate(T_ROLLED):
            at = {0: slice(6, 30), 1: slice(0, 24), -1: slice(8, 32)}[upper[k][1]]
            value = ext[TCH[k], i, at]
            edge = pltpu.roll(zf[8 + n, at], 127 - 2 * i, 1)
            if upper[k][2] > 0:
                tl[n, i, at] = jnp.where(lane24 == 0, edge, pltpu.roll(value, 1, 1))
            else:
                tl[n, i, at] = jnp.where(lane24 == 127, edge, pltpu.roll(value, 127, 1))
        return carry

    lax.fori_loop(0, 10, shift, 0, unroll=5)

    def equations(get, put, w, bs):
        centre = [get("fld", (1, f), 0, 0) for f in range(8)]
        p, m, mob, slope = centre[0], centre[1], centre[2:5], centre[5:8]
        mob_w = w[0] * mob[0] + w[1] * mob[1] + w[2] * mob[2]
        slope_w = w[0] * slope[0] + w[1] * slope[1] + w[2] * slope[2]
        zeros = jnp.zeros((8, 128), F32)
        sum_q, sum_t, sum_m = zeros, zeros, zeros
        sum_l = [zeros, zeros, zeros]
        for n, o in enumerate(offsets):
            dx, dy, dz = o
            if o in upper:
                t = get("ext", (TCH[upper.index(o)],), 0, 0)
            else:
                k = upper.index(minus(o))
                if dz:
                    t = get("tl", (T_ROLLED.index(k),), dx, dy)
                else:
                    t = get("ext", (TCH[k],), dx, dy)
            near = [get("fld", (dz + 1, f), dx, dy) for f in range(8)]
            t = t * near[1]
            q = t * (p - near[0])
            mw = w[0] * near[2] + w[1] * near[3] + w[2] * near[4]
            gw = w[0] * near[5] + w[1] * near[6] + w[2] * near[7]
            sum_q = sum_q + q
            sum_t = sum_t + t
            sum_m = sum_m + t * mw
            for c in range(3):
                sum_l[c] = sum_l[c] + q * near[2 + c]
            put("acoef", (n,), q * gw - t * (mob_w + mw))
        d = 1.0 + slope_w * sum_q + mob_w * sum_t + sum_m
        h = zeros
        for c in range(3):
            res = m * (bs[c] + mob[c] * sum_q + sum_l[c])
            put("resv", (c,), res)
            h = h - w[c] * res
        inv = jnp.where(m > 0, relax_weight / d, 0.0)
        put("dinv", (), inv)
        put("x0", (), inv * h)

    def assemble(i, carry):
        for a in (8, 16):
            refs = {"fld": fld, "ext": ext, "tl": tl}

            def get(name, lead, dx, dy, a=a, refs=refs):
                return refs[name][(*lead, i + 1 + dx, slice(a + dy, a + dy + 8))]

            def put(name, lead, value, a=a):
                at = slice(a, a + 8)
                if name == "x0":
                    xs[0, 1, i + 1, at] = value
                elif name == "resv":
                    resv[lead[0], i, a - 8 : a] = value
                else:
                    {"acoef": acoef, "dinv": dinv}[name][(*lead, i, at)] = value

            at = (i, slice(a, a + 8))
            equations(get, put, [wts[(c, *at)] for c in range(3)], [base[(c, *at)] for c in range(3)])
        return carry

    lax.fori_loop(0, 8, assemble, 0, unroll=2)
    out_copies = [pltpu.make_async_copy(resv, res_out, out_sem.at[0]), pltpu.make_async_copy(xv, x_out, out_sem.at[1])]
    out_copies[0].start()

    rest[1]()

    for row in (7, 24):
        def get(name, lead, dx, dy, row=row):
            if name == "ext":
                return ext[(*lead, *across(1 + dx, row + dy))]
            return {"fld": fld_f, "tl": tl_f}[name][(*lead, *strided(1 + dx, row + dy))]

        def put(name, lead, value, row=row):
            if name == "x0":
                xs[(0, 1, *across(1, row))] = value
            elif name != "resv":
                {"acoef": acoef_f, "dinv": dinv_f}[name][(*lead, *strided(0, row))] = value

        fields, fac, sat, stored = shell[row]
        old = [get("ext", (OM + c,), 0, 0) for c in range(3)]
        equations(get, put, *weights(fields[1], get("ext", (PV,), 0, 0), old, fac, sat, stored))

    pending = []
    for n in range(3):
        wide = n != 1
        lo, hi = (7, 31) if wide else (8, 24)

        acc = jnp.zeros((hi - lo, 128), F32)
        pair = lane24[: hi - lo] // 2
        for x in range(8):
            acc = jnp.where(pair == x, pltpu.roll(xs[n, 1, x + 1, lo:hi], 2 * x + 1, 1), acc)
        px[n, lo:hi] = acc
        start, arrived, left = exchange(messages_x(n, wide), s_x.at[n], r_x.at[n])
        start()
        arrived()
        pending.append(left)
        column = spread([gather(zx[n, 0, d, 6:30], zx[n, 1, d, 6:30]) for d in range(3)], 0)

        for i in range(10):
            value = xs[n, 1, i, 6:30]
            edge = pltpu.roll(column, 127 - 2 * i, 1)
            xs[n, 0, i, 6:30] = jnp.where(lane24 == 0, edge, pltpu.roll(value, 1, 1))
            xs[n, 2, i, 6:30] = jnp.where(lane24 == 127, edge, pltpu.roll(value, 127, 1))

        def relaxed(near, coef, inv, start, value):
            total = jnp.zeros((8, 128), F32)
            for k, o in enumerate(offsets):
                total = total + coef(k) * near(*o)
            return start + (1.0 - relax_weight) * value - inv * total

        def sweep(i, carry, n=n, relaxed=relaxed):
            for a in (8, 16):
                at = slice(a, a + 8)
                value = relaxed(
                    lambda dx, dy, dz: xs[n, dz + 1, i + 1 + dx, a + dy : a + dy + 8],
                    lambda k: acoef[k, i, at],
                    dinv[i, at],
                    xs[0, 1, i + 1, at],
                    xs[n, 1, i + 1, at],
                )
                if n == 2:
                    xv[i, a - 8 : a] = value
                else:
                    xs[n + 1, 1, i + 1, at] = value
            return carry

        lax.fori_loop(0, 8, sweep, 0, unroll=4)
        if n == 1:
            for row in (7, 24):
                xs[(2, 1, *across(1, row))] = relaxed(
                    lambda dx, dy, dz: xs[(1, dz + 1, *across(1 + dx, row + dy))],
                    lambda k: acoef_f[(k, *strided(0, row))],
                    dinv_f[strided(0, row)],
                    xs[(0, 1, *across(1, row))],
                    xs[(1, 1, *across(1, row))],
                )

    out_copies[1].start()
    state[2]()
    rest[2]()
    for left in pending:
        left()
    for c in out_copies:
        c.wait()


def body(cs, om, pv, tr, am, rg, b_tab, c_tab, v_tab):
    anywhere = pl.BlockSpec(memory_space=pltpu.HBM)
    vmem = lambda *s: pltpu.VMEM(s, F32)
    dma = lambda *s: pltpu.SemaphoreType.DMA(s)
    return pl.pallas_call(
        kernel,
        out_shape=(
            jax.ShapeDtypeStruct((3, 8, 16, 128), F32),
            jax.ShapeDtypeStruct((8, 16, 128), F32),
        ),
        in_specs=[anywhere] * 9,
        out_specs=(anywhere,) * 2,
        scratch_shapes=[
            *[pltpu.SMEM((3, 8), F32)] * 3,
            vmem(NCH, NP, NR, 128),
            pltpu.VMEM((2, 8, 16, 128), jnp.int32),
            vmem(3, 8, NP, NR, 128),
            vmem(len(T_ROLLED), NP, NR, 128),
            vmem(3, 8, NR, 128),
            vmem(3, 8, NR, 128),
            vmem(26, 8, NR, 128),
            vmem(8, NR, 128),
            vmem(3, 3, NP, NR, 128),
            vmem(3, NR, 128),
            vmem(3, 2, 3, NR, 128),
            vmem(2, NR, 128),
            vmem(2, 3, 2, NR, 128),
            vmem(8 + len(T_ROLLED), NR, 128),
            vmem(3, 8, 16, 128),
            vmem(8, 16, 128),
            dma(12),
            dma(2),
            dma(28),
            dma(28),
            dma(3),
            dma(3),
            dma(3, 26),
            dma(3, 26),
        ],
        compiler_params=pltpu.CompilerParams(
            collective_id=0, has_side_effects=True, vmem_limit_bytes=60 * 1024 * 1024
        ),
    )(cs, om, pv, tr, am, rg, b_tab, c_tab, v_tab)


def solution(mesh):
    four = P(None, "gx", "gy", "gz")
    three = P("gx", "gy", "gz")
    return jax.shard_map(
        body,
        mesh=mesh,
        in_specs=(four, four, three, four, three, three, P(), P(), P()),
        out_specs=(four, three),
        check_vma=False,
    )
```
